32 devices in a mesh: pos: 8 (over y, x, core), tile: 4 (over z).
Axes of the slice: x: 2, y: 2, z: 4, core: 2. Of those that a mesh axis runs over, the one named last changes fastest.
Arguments:
- obj_tiles: bfloat16 [192, 4, 4096], P('pos'), may hold values from -4.1875 to 4.1875
- tile_map: int32 [32, 6], replicated, may hold values from 0 to 191, as said below
- offsets: int32 [32, 2], replicated, may hold values from 1 to 1919, as said below
- probe: float32 [2, 128, 128], replicated, may hold values from -6 to 6
- intens: float32 [32, 128, 128], P(('pos', 'tile')), may hold values from 0.05 to 2
Outputs:
- obj_grad: float32 [192, 4, 4096], P('pos')
- probe_grad: float32 [2, 128, 128], replicated
The draws below stay inside these ranges and needn't reach their ends.
Inputs may be any that keep to these rules, and one draw needn't show every extreme that they name: tile_map holds every storage index once. A tile's owner is its storage index // 24; the owner depends only on the tile row mod 8 and the tile column mod 1, and different such classes have different owners. `offsets`: every patch lies inside the window, and neither its row nor its column offset is a multiple of 64.
All inputs are finite; a program needn't handle non-finite values.
Results may differ from the reference program's by a relative error of at most 0.0023.
Values may be sent and summed in bfloat16 or wider, within the bound.
A program may use at most 64 MiB of HBM per device.

```python
import math
import jax
import jax.numpy as jnp
from jax import lax

PROBE = 128
TS = 64
SPAN = 3
OWN_R = 8
OWN_C = 1
BLK_C = 6
TILE_DEV = 24
TR = 32
TC = 6
NTILE = 192
NPOS = 32


def draw_offsets(key, part):
    key_rows, key_cols, key_fine_r, key_fine_c = jax.random.split(key, 4)
    tile_rows = jax.random.randint(key_rows, (NPOS,), 0, TR - SPAN + 1)
    tile_cols = jax.random.randint(key_cols, (NPOS,), 0, TC - SPAN + 1)
    fine_rows = jax.random.randint(key_fine_r, (NPOS,), 1, TS)
    fine_cols = jax.random.randint(key_fine_c, (NPOS,), 1, TS)
    tile_rows = tile_rows.at[0].set(0).at[NPOS - 1].set(TR - SPAN)
    tile_cols = tile_cols.at[0].set(0).at[NPOS - 1].set(TC - SPAN)
    fine_rows = fine_rows.at[0].set(1).at[NPOS - 1].set(TS - 1)
    fine_cols = fine_cols.at[0].set(1).at[NPOS - 1].set(TS - 1)
    return jnp.stack([tile_rows * TS + fine_rows, tile_cols * TS + fine_cols], axis=1).astype(jnp.int32)


def draw_tile_map(key, part):
    key_rows, key_cols, key_slots = jax.random.split(key, 3)
    row_perm = jax.random.permutation(key_rows, OWN_R).astype(jnp.int32)
    col_perm = jax.random.permutation(key_cols, OWN_C).astype(jnp.int32)
    slot_perm = jax.random.permutation(key_slots, TILE_DEV).astype(jnp.int32)
    grid_r = jnp.arange(TR, dtype=jnp.int32)[:, None]
    grid_c = jnp.arange(TC, dtype=jnp.int32)[None, :]
    owner_id = row_perm[grid_r % OWN_R] * OWN_C + col_perm[grid_c % OWN_C]
    local_id = slot_perm[grid_r // OWN_R * BLK_C + grid_c // OWN_C]
    return (owner_id * TILE_DEV + local_id).astype(jnp.int32)


def steps_of(own_key, shape, shards, smallest, largest):
    loudness, own = 1.0, jax.random.fold_in(own_key, 6)
    for dim, shards_of in shards:
        heights = jnp.exp(jax.random.uniform(jax.random.fold_in(own, dim), (shards_of,), jnp.float32, smallest / len(shards), largest / len(shards)))
        loudness = loudness * jnp.repeat(heights, shape[dim] // shards_of).reshape([-1 if axis == dim else 1 for axis in range(len(shape))])
    return loudness


def gaussian(own_key, extent, scale, reach, cuts=(), kind=jnp.bfloat16):
    drawn = scale * jax.random.normal(own_key, extent, jnp.float32)
    if cuts:
        drawn = drawn * steps_of(own_key, extent, cuts, -0.22, 0.18)
    return jnp.clip(drawn, -reach, reach).astype(kind)


def setup_inputs(seed: int = 0) -> dict:
    key_list = jax.random.split(jax.random.key(seed), 6)
    return {
        "obj_tiles": gaussian(key_list[0], (NTILE, 4, TS * TS), 0.7, 4.1875, ((0, 8),)),
        "tile_map": draw_tile_map(jax.random.fold_in(key_list[5], 71), 0),
        "offsets": draw_offsets(jax.random.fold_in(key_list[5], 71), 0),
        "probe": gaussian(key_list[3], (2, PROBE, PROBE), 1.0, 6.0, (), jnp.float32),
        "intens": jnp.clip(jnp.exp(math.log(2.0) - 3.6888794 * jax.random.uniform(key_list[4], (NPOS, PROBE, PROBE), jnp.float32) ** steps_of(key_list[4], (NPOS, PROBE, PROBE), ((0, 32),), -0.2, 0.2)), 0.05, 2.0),
    }


def propagator_phase(width_px):
    positions = jnp.arange(width_px, dtype=jnp.int32)
    centred = (positions + width_px // 2) % width_px - width_px // 2
    square = (centred * centred).astype(jnp.float32)
    return (square[:, None] + square[None, :]) * (-0.2 / width_px)


def forward_ft(field):
    return jnp.fft.fft2(field, norm="ortho")


def inverse_ft(field):
    return jnp.fft.ifft2(field, norm="ortho")


def reference(obj_tiles, tile_map, offsets, probe, intens):
    grid_rows, grid_cols = tile_map.shape
    n_comps = obj_tiles.shape[1]
    arranged = obj_tiles[tile_map.reshape(-1)].astype(jnp.float32)
    window_img = arranged.reshape(grid_rows, grid_cols, n_comps, TS, TS).transpose(2, 0, 3, 1, 4).reshape(n_comps, grid_rows * TS, grid_cols * TS)
    angles = propagator_phase(PROBE)
    kernel = lax.complex(jnp.cos(angles), jnp.sin(angles))
    probe_c = lax.complex(probe[0], probe[1])
    zero_idx = jnp.zeros((), jnp.int32)

    def accumulate(position, state_pair):
        grad_img, probe_acc = state_pair
        corner = offsets[position].astype(jnp.int32)
        start_at = (zero_idx, corner[0], corner[1])
        patch_px = lax.dynamic_slice(window_img, start_at, (n_comps, PROBE, PROBE))
        entry_wave = lax.complex(patch_px[0], patch_px[1])
        exit_wave = lax.complex(patch_px[2], patch_px[3])
        spread = inverse_ft(kernel * forward_ft(probe_c * entry_wave))
        far_field = forward_ft(spread * exit_wave)
        excess = far_field.real * far_field.real + far_field.imag * far_field.imag - intens[position]
        back_wave = inverse_ft(excess * far_field)
        grad_exit = jnp.conj(spread) * back_wave
        inner_wave = inverse_ft(jnp.conj(kernel) * forward_ft(jnp.conj(exit_wave) * back_wave))
        grad_entry = jnp.conj(probe_c) * inner_wave
        grad_probe = jnp.conj(entry_wave) * inner_wave
        rounded = jnp.stack([grad_entry.real, grad_entry.imag, grad_exit.real, grad_exit.imag]).astype(jnp.bfloat16)
        rounded = lax.optimization_barrier(rounded).astype(jnp.float32)
        current = lax.dynamic_slice(grad_img, start_at, (n_comps, PROBE, PROBE))
        grad_img = lax.dynamic_update_slice(grad_img, current + rounded, start_at)
        probe_acc = probe_acc + jnp.stack([grad_probe.real, grad_probe.imag])
        return grad_img, probe_acc

    grad_init = jnp.zeros(window_img.shape, jnp.float32)
    probe_init = jnp.zeros((2, PROBE, PROBE), jnp.float32)
    grad_img, probe_acc = lax.fori_loop(0, NPOS, accumulate, (grad_init, probe_init))
    blocks = grad_img.reshape(n_comps, grid_rows, TS, grid_cols, TS).transpose(1, 3, 0, 2, 4).reshape(grid_rows * grid_cols, n_comps, TS * TS)
    obj_grad = jnp.zeros_like(blocks).at[tile_map.reshape(-1)].set(blocks)
    return obj_grad, probe_acc
```

```python
import functools
import math

import jax
import jax.numpy as jnp
import numpy as np
from jax import lax
from jax.experimental import pallas as pl
from jax.experimental.pallas import tpu as pltpu
from jax.sharding import PartitionSpec as P

TS = 64
OWN_R = 8


def matmul_hi(left_op, right_op):
    return jnp.dot(
        left_op, right_op, precision=lax.Precision.HIGHEST, preferred_element_type=jnp.float32
    )


def spectral_tables(width_px):
    positions = jnp.arange(width_px, dtype=jnp.int32)
    phase_idx = positions[:, None] * positions[None, :] % width_px
    angles = phase_idx.astype(jnp.float32) * (2.0 * math.pi / width_px)
    norm_factor = 1.0 / math.sqrt(width_px)
    return (jnp.cos(angles) * norm_factor, -jnp.sin(angles) * norm_factor)


def complex_matmul(left_re, left_im, right_re, right_im):
    out_re = matmul_hi(left_re, right_re) - matmul_hi(left_im, right_im)
    out_im = matmul_hi(left_re, right_im) + matmul_hi(left_im, right_re)
    return (out_re, out_im)


def propagation_matrix(width_px, fwd_re, fwd_im, sign_val):
    positions = jnp.arange(width_px, dtype=jnp.int32)
    centred = (positions + width_px // 2) % width_px - width_px // 2
    angles = (centred * centred).astype(jnp.float32) * (-0.2 / width_px) * sign_val
    phase_re = jnp.cos(angles)[:, None]
    phase_im = jnp.sin(angles)[:, None]
    scaled_re = phase_re * fwd_re - phase_im * fwd_im
    scaled_im = phase_re * fwd_im + phase_im * fwd_re
    return complex_matmul(fwd_re, -fwd_im, scaled_re, scaled_im)


def transform(part_re, part_im, table_re, table_im):
    mid_re, mid_im = complex_matmul(part_re, part_im, table_re, table_im)
    return complex_matmul(table_re, table_im, mid_re, mid_im)


def product(left_re, left_im, right_re, right_im):
    return (left_re * right_re - left_im * right_im, left_re * right_im + left_im * right_re)


def pick(table, ids):
    rows = jnp.arange(table.shape[0], dtype=jnp.int32)
    chooser = (ids.reshape(-1)[:, None] == rows[None, :]).astype(table.dtype)
    flat = jnp.dot(
        chooser, table.reshape(table.shape[0], -1), preferred_element_type=jnp.float32
    ).astype(table.dtype)
    return flat.reshape(ids.shape + table.shape[1:])


def general_plan(obj_tiles, tile_map, offsets, probe, intens):
    owners = lax.axis_size("pos")
    layers = lax.axis_size("tile")
    me_pos = lax.axis_index("pos")
    me_tile = lax.axis_index("tile")
    tiles_dev = obj_tiles.shape[0]
    tile_edge = TS
    width_px = probe.shape[-1]
    tile_span = width_px // tile_edge + 1
    cols_own = owners // OWN_R
    cols_cap = (tile_span + cols_own - 1) // cols_own
    slots = (tile_span + OWN_R - 1) // OWN_R * cols_cap
    span_idx = jnp.arange(tile_span, dtype=jnp.int32)
    slot_grid = (span_idx[:, None] // OWN_R * cols_cap + span_idx[None, :] // cols_own).reshape(-1)

    def footprint(corner):
        row_ids = corner[0] // tile_edge + span_idx
        col_ids = corner[1] // tile_edge + span_idx
        store_id = tile_map[row_ids[:, None], col_ids[None, :]].reshape(-1)
        owner_id = store_id // tiles_dev
        return (owner_id, store_id - owner_id * tiles_dev)

    by_device = offsets.reshape(owners, layers, 2)
    peer_corners = lax.dynamic_index_in_dim(by_device, me_tile, 1, keepdims=False)
    peer_owner, peer_local = jax.vmap(footprint)(peer_corners)
    slot_ids = jnp.arange(slots, dtype=jnp.int32)
    matches = (peer_owner == me_pos)[:, :, None] & (
        slot_grid[None, :, None] == slot_ids[None, None, :]
    )
    send_local = jnp.sum(jnp.where(matches, peer_local[:, :, None], 0), axis=1)
    send_live = jnp.any(matches, axis=1)
    chosen = jnp.where(
        send_live[:, :, None, None], pick(obj_tiles, send_local), jnp.zeros((), obj_tiles.dtype)
    )
    my_corner = lax.dynamic_index_in_dim(offsets, me_pos * layers + me_tile, 0, keepdims=False)
    my_owner, my_local = footprint(my_corner)
    flat_slot = my_owner * slots + slot_grid
    inner_y = my_corner[0] % tile_edge
    inner_x = my_corner[1] % tile_edge
    zero_idx = jnp.zeros((), jnp.int32)
    fwd_re, fwd_im = spectral_tables(width_px)
    ahead_re, ahead_im = propagation_matrix(width_px, fwd_re, fwd_im, 1.0)
    behind_re, behind_im = propagation_matrix(width_px, fwd_re, fwd_im, -1.0)
    probe_re = probe[0]
    probe_im = probe[1]
    received = lax.all_to_all(chosen, "pos", split_axis=0, concat_axis=0, tiled=True)
    n_comps = received.shape[2]
    pieces = pick(
        received.reshape(owners * slots, n_comps, tile_edge * tile_edge), flat_slot
    )
    region = pieces.reshape(tile_span, tile_span, n_comps, tile_edge, tile_edge).transpose(
        2, 0, 3, 1, 4
    )
    region = region.reshape(n_comps, tile_span * tile_edge, tile_span * tile_edge)
    patch_px = lax.dynamic_slice(
        region, (zero_idx, inner_y, inner_x), (n_comps, width_px, width_px)
    )
    fetched = patch_px.astype(jnp.float32)
    entry_patch = fetched[:2]
    leaving = fetched[2:]
    first_re, first_im = product(probe_re, probe_im, entry_patch[0], entry_patch[1])
    spread_re, spread_im = transform(first_re, first_im, ahead_re, ahead_im)
    second_re, second_im = product(spread_re, spread_im, leaving[0], leaving[1])
    far_re, far_im = transform(second_re, second_im, fwd_re, fwd_im)
    excess = far_re * far_re + far_im * far_im - intens[0]
    back_re, back_im = transform(excess * far_re, excess * far_im, fwd_re, -fwd_im)
    exit_re, exit_im = product(spread_re, -spread_im, back_re, back_im)
    mid_re, mid_im = product(leaving[0], -leaving[1], back_re, back_im)
    inner_re, inner_im = transform(mid_re, mid_im, behind_re, behind_im)
    entry_re, entry_im = product(probe_re, -probe_im, inner_re, inner_im)
    grad_re, grad_im = product(entry_patch[0], -entry_patch[1], inner_re, inner_im)
    patch_grad = jnp.stack([entry_re, entry_im, exit_re, exit_im]).astype(jnp.bfloat16)
    region = jnp.zeros((4, tile_span * tile_edge, tile_span * tile_edge), jnp.bfloat16)
    region = lax.dynamic_update_slice(region, patch_grad, (zero_idx, inner_y, inner_x))
    pieces = region.reshape(4, tile_span, tile_edge, tile_span, tile_edge).transpose(1, 3, 0, 2, 4)
    pieces = pieces.reshape(tile_span * tile_span, 4, tile_edge * tile_edge)
    outgoing = (
        jnp.zeros((owners * slots, 4, tile_edge * tile_edge), jnp.bfloat16)
        .at[flat_slot]
        .set(pieces)
    )
    outgoing = outgoing.reshape(owners, slots, 4, tile_edge * tile_edge)
    returned = lax.all_to_all(outgoing, "pos", split_axis=0, concat_axis=0, tiled=True)
    tile_ids = jnp.arange(tiles_dev, dtype=jnp.int32)
    selector = (
        (send_local.reshape(-1)[None, :] == tile_ids[:, None]) & send_live.reshape(-1)[None, :]
    ).astype(jnp.bfloat16)
    local_sum = jnp.dot(
        selector,
        returned.reshape(owners * slots, 4 * tile_edge * tile_edge),
        preferred_element_type=jnp.float32,
    )
    probe_part = jnp.stack([grad_re, grad_im])
    tile_total, probe_layer = lax.psum((local_sum, probe_part), "tile")
    probe_total = lax.psum(probe_layer, "pos")
    return (tile_total.reshape(tiles_dev, 4, tile_edge * tile_edge), probe_total)


MESH = pl.DeviceIdType.MESH
VM = pltpu.VMEM
SM = pltpu.SMEM


def one_hot(rows, cols, shift):
    row = lax.broadcasted_iota(jnp.int32, (rows, cols), 0)
    col = lax.broadcasted_iota(jnp.int32, (rows, cols), 1)
    return jnp.where(col == row + shift, 1.0, 0.0).astype(jnp.bfloat16)


def bdot(a, b):
    return jnp.dot(a, b, preferred_element_type=jnp.float32)


def class_of(tmap, me, per):
    found = jnp.int32(0)
    for r in range(OWN_R):
        found = jnp.where(lax.div(tmap[r, 0], per) == me, r, found)
    return found


def place(off, n, rho):
    y = off[n, 0]
    x = off[n, 1]
    ty = lax.div(y, TS)
    tx = lax.div(x, TS)
    step = lax.rem(rho - ty + 64 * OWN_R, OWN_R)
    return ty + step, tx, x - tx * TS, step < 3


def pack_kernel(owners, layers, per, off, tmap, tiles, slots):
    me = lax.axis_index("pos")
    z = lax.axis_index("tile")
    rho = class_of(tmap, me, per)
    for p in range(owners):
        row, tx, ix, live = place(off, p * layers + z, rho)

        @pl.when(live)
        def _():
            acc = None
            for j in range(3):
                local = tmap[row, tx + j] - me * per
                part = bdot(tiles[local], one_hot(TS, 2 * TS, TS * j - ix))
                acc = part if acc is None else acc + part
            slots[p] = acc.astype(jnp.bfloat16)


def fetch_kernel(owners, slots, got, send_sem, recv_sem, own_sem):
    me = lax.axis_index("pos")
    z = lax.axis_index("tile")
    barrier = pltpu.get_barrier_semaphore()
    for d in range(1, owners):
        peer = lax.rem(me + d, owners)
        pl.semaphore_signal(barrier, inc=1, device_id=(peer, z), device_id_type=MESH)
    own = pltpu.make_async_copy(slots.at[me], got.at[me], own_sem)
    own.start()
    pl.semaphore_wait(barrier, owners - 1)
    copies = []
    for d in range(1, owners):
        peer = lax.rem(me + d, owners)
        copy = pltpu.make_async_remote_copy(
            src_ref=slots.at[peer],
            dst_ref=got.at[me],
            send_sem=send_sem.at[d],
            recv_sem=recv_sem.at[d],
            device_id=(peer, z),
            device_id_type=MESH,
        )
        copy.start()
        copies.append(copy)
    own.wait()
    for copy in copies:
        copy.wait()


def split(a):
    high = a.astype(jnp.bfloat16)
    return high, (a - high.astype(jnp.float32)).astype(jnp.bfloat16)


def rmul(a, table):
    high, low = split(a)
    return bdot(high, table[0]) + (bdot(low, table[0]) + bdot(high, table[1]))


def lmul(table, a):
    high, low = split(a)
    return bdot(table[0], high) + (bdot(table[0], low) + bdot(table[1], high))


def both_sides(re, im, right, left):
    width = re.shape[1]
    mid = rmul(jnp.concatenate([re, im], axis=1), right)
    out = lmul(left, jnp.concatenate([mid[:, :width], mid[:, width:]], axis=0))
    return out[:width], out[width:]


def wave_kernel(layers, per, off, tmap, got, probe, intens, tables, slots, pgrad):
    n = lax.axis_index("pos") * layers + lax.axis_index("tile")
    y = off[n, 0]
    ty = lax.div(y, TS)
    iy = y - ty * TS
    w = probe.shape[-1]
    owner = [lax.div(tmap[ty + s, 0], per) for s in range(3)]
    rows = []
    for s in range(3):
        block = got[owner[s]]
        rows.append(jnp.concatenate([block[k * TS : (k + 1) * TS] for k in range(4)], axis=1))
    patch = bdot(one_hot(w, 3 * TS, iy), jnp.concatenate(rows, axis=0))
    en_re, en_im, ex_re, ex_im = (patch[:, k * w : (k + 1) * w] for k in range(4))
    pr, pi = probe[0], probe[1]
    fw, fc, aw, ac = ((tables[2 * i], tables[2 * i + 1]) for i in range(4))
    re, im = product(pr, pi, en_re, en_im)
    sp_re, sp_im = both_sides(re, im, aw, ac)
    re, im = product(sp_re, sp_im, ex_re, ex_im)
    far_re, far_im = both_sides(re, im, fw, fc)
    excess = far_re * far_re + far_im * far_im - intens[0]
    bk_re, bk_im = both_sides(excess * far_re, excess * far_im, fc, fw)
    gx_re, gx_im = product(sp_re, -sp_im, bk_re, bk_im)
    re, im = product(ex_re, -ex_im, bk_re, bk_im)
    in_re, in_im = both_sides(re, im, ac, aw)
    ge_re, ge_im = product(pr, -pi, in_re, in_im)
    gp_re, gp_im = product(en_re, -en_im, in_re, in_im)
    pgrad[0:w] = gp_re
    pgrad[w : 2 * w] = gp_im
    grad = jnp.concatenate([ge_re, ge_im, gx_re, gx_im], axis=1).astype(jnp.bfloat16)
    region = bdot(one_hot(3 * TS, w, -iy), grad).astype(jnp.bfloat16)
    for s in range(3):
        for k in range(4):
            slots[owner[s], k * TS : (k + 1) * TS, :] = region[
                s * TS : (s + 1) * TS, k * w : (k + 1) * w
            ]


def spread_kernel(
    owners, layers, slots, pgrad, got, ptotal, part, summed, layer_part,
    own_sem, a_send, a_recv, up_send, up_recv, dn_send, dn_recv,
    p_send, p_recv, q_send, q_recv, r_send, r_recv,
):
    me = lax.axis_index("pos")
    z = lax.axis_index("tile")
    chunk = pgrad.shape[0] // owners

    def remote(src, dst, ssem, rsem, p, t):
        return pltpu.make_async_remote_copy(
            src_ref=src, dst_ref=dst, send_sem=ssem, recv_sem=rsem,
            device_id=(p, t), device_id_type=MESH,
        )

    barrier = pltpu.get_barrier_semaphore()
    for d in range(1, owners):
        pl.semaphore_signal(
            barrier, inc=1, device_id=(lax.rem(me + d, owners), z), device_id_type=MESH
        )
    for d in range(1, layers):
        pl.semaphore_signal(
            barrier, inc=1, device_id=(me, lax.rem(z + d, layers)), device_id_type=MESH
        )
    own = pltpu.make_async_copy(slots.at[me], got.at[z, me], own_sem)
    own.start()
    pl.semaphore_wait(barrier, owners + layers - 2)

    probes, shares = [], []
    for d in range(1, owners):
        peer = lax.rem(me + d, owners)
        probes.append(
            remote(
                pgrad.at[pl.ds(pl.multiple_of(peer * chunk, chunk), chunk)],
                part.at[me], p_send.at[d], p_recv.at[d], peer, z,
            )
        )
        probes[-1].start()
    for d in range(1, owners):
        peer = lax.rem(me + d, owners)
        shares.append(remote(slots.at[peer], got.at[z, me], a_send.at[d], a_recv.at[d], peer, z))
        shares[-1].start()

    def up(t, p, item, target):
        ref = got.at[item, p]
        return remote(ref, ref, up_send.at[t, p], up_recv.at[t, p], me, target)

    def down(t, p, item, target):
        ref = got.at[item, p]
        return remote(ref, ref, dn_send.at[t, p], dn_recv.at[t, p], me, target)

    def first(p):
        @pl.when(z < layers - 1)
        def _():
            up(0, p, z, z + 1).start()

        @pl.when(z > 0)
        def _():
            down(0, p, z, z - 1).start()

    own.wait()
    first(me)
    part[me] = pgrad[pl.ds(pl.multiple_of(me * chunk, chunk), chunk)]
    for copy in probes:
        copy.wait()
    summed[...] = jnp.sum(part[...], axis=0)
    layer_part[z] = summed[...]
    zs = []
    for d in range(1, layers):
        zs.append(
            remote(
                summed, layer_part.at[z], q_send.at[d], q_recv.at[d],
                me, lax.rem(z + d, layers),
            )
        )
        zs[-1].start()
    for d in range(1, owners):
        shares[d - 1].wait_recv()
        first(lax.rem(me - d + owners, owners))
    for copy in zs:
        copy.wait()
    ptotal[me] = jnp.sum(layer_part[...], axis=0)
    outs = []
    for d in range(1, owners):
        outs.append(
            remote(
                ptotal.at[me], ptotal.at[me], r_send.at[d], r_recv.at[d],
                lax.rem(me + d, owners), z,
            )
        )
        outs[-1].start()

    for t in range(layers - 1):
        @pl.loop(0, owners)
        def _(i):
            p = lax.rem(me - i + owners, owners)

            @pl.when(z - 1 - t >= 0)
            def _():
                up(t, p, z - 1 - t, z - 1).wait_recv()
                if t < layers - 2:

                    @pl.when(z < layers - 1)
                    def _():
                        up(t + 1, p, z - 1 - t, z + 1).start()

            @pl.when(z + 1 + t <= layers - 1)
            def _():
                down(t, p, z + 1 + t, z + 1).wait_recv()
                if t < layers - 2:

                    @pl.when(z > 0)
                    def _():
                        down(t + 1, p, z + 1 + t, z - 1).start()

    for copy in shares:
        copy.wait_send()
    for copy in outs:
        copy.wait()
    for t in range(layers - 1):
        @pl.loop(0, owners)
        def _(p):
            @pl.when((z - t >= 0) & (z < layers - 1))
            def _():
                up(t, p, z - t, z + 1).wait_send()

            @pl.when((z + t <= layers - 1) & (z > 0))
            def _():
                down(t, p, z + t, z - 1).wait_send()


def add_kernel(owners, layers, per, off, tmap, got, out):
    me = lax.axis_index("pos")
    rho = class_of(tmap, me, per)
    out[...] = jnp.zeros_like(out)

    @pl.loop(0, owners * layers)
    def _(n):
        row, tx, ix, live = place(off, n, rho)

        @pl.when(live)
        def _():
            block = got[lax.rem(n, layers), lax.div(n, layers)]
            for j in range(3):
                local = tmap[row, tx + j] - me * per
                out[local] += bdot(block, one_hot(2 * TS, TS, ix - TS * j))


def spectral_blocks(width):
    k = np.arange(width)
    fwd = np.exp(-2j * np.pi * (np.outer(k, k) % width) / width) / np.sqrt(width)
    centred = (k + width // 2) % width - width // 2
    phase = np.exp(-0.2j * centred * centred / width)
    ahead = np.conj(fwd) @ (phase[:, None] * fwd)
    found = []
    for m in (fwd, np.conj(fwd), ahead, np.conj(ahead)):
        full = np.block([[m.real, m.imag], [-m.imag, m.real]]).astype(np.float32)
        high = full.astype(jnp.bfloat16)
        found += [high, (full - high.astype(np.float32)).astype(jnp.bfloat16)]
    return np.stack(found)


def params(**kw):
    return pltpu.CompilerParams(vmem_limit_bytes=32 * 1024 * 1024, **kw)


def row_plan(obj_tiles, tile_map, offsets, probe, intens):
    owners = lax.axis_size("pos")
    layers = lax.axis_size("tile")
    per = obj_tiles.shape[0]
    w = probe.shape[-1]
    bf, f32 = jnp.bfloat16, jnp.float32
    vm = pl.BlockSpec(memory_space=VM)
    sm = pl.BlockSpec(memory_space=SM)
    dma = pltpu.SemaphoreType.DMA
    tiles = obj_tiles.reshape(per, 4 * TS, TS)
    slot_shape = jax.ShapeDtypeStruct((owners, 4 * TS, w), bf)
    slots = pl.pallas_call(
        functools.partial(pack_kernel, owners, layers, per),
        out_shape=slot_shape,
        in_specs=[sm, sm, vm],
        out_specs=vm,
        compiler_params=params(),
    )(offsets, tile_map, tiles)
    got = pl.pallas_call(
        functools.partial(fetch_kernel, owners),
        out_shape=slot_shape,
        in_specs=[vm],
        out_specs=vm,
        scratch_shapes=[dma((owners,)), dma((owners,)), dma],
        compiler_params=params(collective_id=0, has_side_effects=True),
    )(slots)
    tables = jnp.asarray(spectral_blocks(w))
    grads, pgrad = pl.pallas_call(
        functools.partial(wave_kernel, layers, per),
        out_shape=[slot_shape, jax.ShapeDtypeStruct((2 * w, w), f32)],
        in_specs=[sm, sm, vm, vm, vm, vm],
        out_specs=[vm, vm],
        compiler_params=params(),
    )(offsets, tile_map, got, probe, intens, tables)
    chunk = 2 * w // owners
    spread, ptotal = pl.pallas_call(
        functools.partial(spread_kernel, owners, layers),
        out_shape=[
            jax.ShapeDtypeStruct((layers, owners, 4 * TS, w), bf),
            jax.ShapeDtypeStruct((owners, chunk, w), f32),
        ],
        in_specs=[vm, vm],
        out_specs=[vm, vm],
        scratch_shapes=[
            VM((owners, chunk, w), f32), VM((chunk, w), f32), VM((layers, chunk, w), f32), dma,
            dma((owners,)), dma((owners,)),
            dma((layers, owners)), dma((layers, owners)), dma((layers, owners)), dma((layers, owners)),
            dma((owners,)), dma((owners,)), dma((layers,)), dma((layers,)), dma((owners,)), dma((owners,)),
        ],
        compiler_params=params(collective_id=1, has_side_effects=True),
    )(grads, pgrad)
    total = pl.pallas_call(
        functools.partial(add_kernel, owners, layers, per),
        out_shape=jax.ShapeDtypeStruct((per, 4 * TS, TS), f32),
        in_specs=[sm, sm, vm],
        out_specs=vm,
        compiler_params=params(),
    )(offsets, tile_map, spread)
    return (total.reshape(per, 4, TS * TS), ptotal.reshape(2, w, w))


def solution(mesh):
    in_specs = (P("pos", None, None), P(), P(), P(), P(("pos", "tile"), None, None))
    out_specs = (P("pos", None, None), P())
    plan = row_plan if mesh.shape["pos"] == OWN_R else general_plan
    return jax.shard_map(plan, mesh=mesh, in_specs=in_specs, out_specs=out_specs, check_vma=False)
```

```python
import functools
import math

import jax
import jax.numpy as jnp
import numpy as np
from jax import lax
from jax.experimental import pallas as pl
from jax.experimental.pallas import tpu as pltpu
from jax.sharding import PartitionSpec as P

TS = 64
OWN_R = 8


def matmul_hi(left_op, right_op):
    return jnp.dot(
        left_op, right_op, precision=lax.Precision.HIGHEST, preferred_element_type=jnp.float32
    )


def spectral_tables(width_px):
    positions = jnp.arange(width_px, dtype=jnp.int32)
    phase_idx = positions[:, None] * positions[None, :] % width_px
    angles = phase_idx.astype(jnp.float32) * (2.0 * math.pi / width_px)
    norm_factor = 1.0 / math.sqrt(width_px)
    return (jnp.cos(angles) * norm_factor, -jnp.sin(angles) * norm_factor)


def complex_matmul(left_re, left_im, right_re, right_im):
    out_re = matmul_hi(left_re, right_re) - matmul_hi(left_im, right_im)
    out_im = matmul_hi(left_re, right_im) + matmul_hi(left_im, right_re)
    return (out_re, out_im)


def propagation_matrix(width_px, fwd_re, fwd_im, sign_val):
    positions = jnp.arange(width_px, dtype=jnp.int32)
    centred = (positions + width_px // 2) % width_px - width_px // 2
    angles = (centred * centred).astype(jnp.float32) * (-0.2 / width_px) * sign_val
    phase_re = jnp.cos(angles)[:, None]
    phase_im = jnp.sin(angles)[:, None]
    scaled_re = phase_re * fwd_re - phase_im * fwd_im
    scaled_im = phase_re * fwd_im + phase_im * fwd_re
    return complex_matmul(fwd_re, -fwd_im, scaled_re, scaled_im)


def transform(part_re, part_im, table_re, table_im):
    mid_re, mid_im = complex_matmul(part_re, part_im, table_re, table_im)
    return complex_matmul(table_re, table_im, mid_re, mid_im)


def product(left_re, left_im, right_re, right_im):
    return (left_re * right_re - left_im * right_im, left_re * right_im + left_im * right_re)


def pick(table, ids):
    rows = jnp.arange(table.shape[0], dtype=jnp.int32)
    chooser = (ids.reshape(-1)[:, None] == rows[None, :]).astype(table.dtype)
    flat = jnp.dot(
        chooser, table.reshape(table.shape[0], -1), preferred_element_type=jnp.float32
    ).astype(table.dtype)
    return flat.reshape(ids.shape + table.shape[1:])


def general_plan(obj_tiles, tile_map, offsets, probe, intens):
    owners = lax.axis_size("pos")
    layers = lax.axis_size("tile")
    me_pos = lax.axis_index("pos")
    me_tile = lax.axis_index("tile")
    tiles_dev = obj_tiles.shape[0]
    tile_edge = TS
    width_px = probe.shape[-1]
    tile_span = width_px // tile_edge + 1
    cols_own = owners // OWN_R
    cols_cap = (tile_span + cols_own - 1) // cols_own
    slots = (tile_span + OWN_R - 1) // OWN_R * cols_cap
    span_idx = jnp.arange(tile_span, dtype=jnp.int32)
    slot_grid = (span_idx[:, None] // OWN_R * cols_cap + span_idx[None, :] // cols_own).reshape(-1)

    def footprint(corner):
        row_ids = corner[0] // tile_edge + span_idx
        col_ids = corner[1] // tile_edge + span_idx
        store_id = tile_map[row_ids[:, None], col_ids[None, :]].reshape(-1)
        owner_id = store_id // tiles_dev
        return (owner_id, store_id - owner_id * tiles_dev)

    by_device = offsets.reshape(owners, layers, 2)
    peer_corners = lax.dynamic_index_in_dim(by_device, me_tile, 1, keepdims=False)
    peer_owner, peer_local = jax.vmap(footprint)(peer_corners)
    slot_ids = jnp.arange(slots, dtype=jnp.int32)
    matches = (peer_owner == me_pos)[:, :, None] & (
        slot_grid[None, :, None] == slot_ids[None, None, :]
    )
    send_local = jnp.sum(jnp.where(matches, peer_local[:, :, None], 0), axis=1)
    send_live = jnp.any(matches, axis=1)
    chosen = jnp.where(
        send_live[:, :, None, None], pick(obj_tiles, send_local), jnp.zeros((), obj_tiles.dtype)
    )
    my_corner = lax.dynamic_index_in_dim(offsets, me_pos * layers + me_tile, 0, keepdims=False)
    my_owner, my_local = footprint(my_corner)
    flat_slot = my_owner * slots + slot_grid
    inner_y = my_corner[0] % tile_edge
    inner_x = my_corner[1] % tile_edge
    zero_idx = jnp.zeros((), jnp.int32)
    fwd_re, fwd_im = spectral_tables(width_px)
    ahead_re, ahead_im = propagation_matrix(width_px, fwd_re, fwd_im, 1.0)
    behind_re, behind_im = propagation_matrix(width_px, fwd_re, fwd_im, -1.0)
    probe_re = probe[0]
    probe_im = probe[1]
    received = lax.all_to_all(chosen, "pos", split_axis=0, concat_axis=0, tiled=True)
    n_comps = received.shape[2]
    pieces = pick(
        received.reshape(owners * slots, n_comps, tile_edge * tile_edge), flat_slot
    )
    region = pieces.reshape(tile_span, tile_span, n_comps, tile_edge, tile_edge).transpose(
        2, 0, 3, 1, 4
    )
    region = region.reshape(n_comps, tile_span * tile_edge, tile_span * tile_edge)
    patch_px = lax.dynamic_slice(
        region, (zero_idx, inner_y, inner_x), (n_comps, width_px, width_px)
    )
    fetched = patch_px.astype(jnp.float32)
    entry_patch = fetched[:2]
    leaving = fetched[2:]
    first_re, first_im = product(probe_re, probe_im, entry_patch[0], entry_patch[1])
    spread_re, spread_im = transform(first_re, first_im, ahead_re, ahead_im)
    second_re, second_im = product(spread_re, spread_im, leaving[0], leaving[1])
    far_re, far_im = transform(second_re, second_im, fwd_re, fwd_im)
    excess = far_re * far_re + far_im * far_im - intens[0]
    back_re, back_im = transform(excess * far_re, excess * far_im, fwd_re, -fwd_im)
    exit_re, exit_im = product(spread_re, -spread_im, back_re, back_im)
    mid_re, mid_im = product(leaving[0], -leaving[1], back_re, back_im)
    inner_re, inner_im = transform(mid_re, mid_im, behind_re, behind_im)
    entry_re, entry_im = product(probe_re, -probe_im, inner_re, inner_im)
    grad_re, grad_im = product(entry_patch[0], -entry_patch[1], inner_re, inner_im)
    patch_grad = jnp.stack([entry_re, entry_im, exit_re, exit_im]).astype(jnp.bfloat16)
    region = jnp.zeros((4, tile_span * tile_edge, tile_span * tile_edge), jnp.bfloat16)
    region = lax.dynamic_update_slice(region, patch_grad, (zero_idx, inner_y, inner_x))
    pieces = region.reshape(4, tile_span, tile_edge, tile_span, tile_edge).transpose(1, 3, 0, 2, 4)
    pieces = pieces.reshape(tile_span * tile_span, 4, tile_edge * tile_edge)
    outgoing = (
        jnp.zeros((owners * slots, 4, tile_edge * tile_edge), jnp.bfloat16)
        .at[flat_slot]
        .set(pieces)
    )
    outgoing = outgoing.reshape(owners, slots, 4, tile_edge * tile_edge)
    returned = lax.all_to_all(outgoing, "pos", split_axis=0, concat_axis=0, tiled=True)
    tile_ids = jnp.arange(tiles_dev, dtype=jnp.int32)
    selector = (
        (send_local.reshape(-1)[None, :] == tile_ids[:, None]) & send_live.reshape(-1)[None, :]
    ).astype(jnp.bfloat16)
    local_sum = jnp.dot(
        selector,
        returned.reshape(owners * slots, 4 * tile_edge * tile_edge),
        preferred_element_type=jnp.float32,
    )
    probe_part = jnp.stack([grad_re, grad_im])
    tile_total, probe_layer = lax.psum((local_sum, probe_part), "tile")
    probe_total = lax.psum(probe_layer, "pos")
    return (tile_total.reshape(tiles_dev, 4, tile_edge * tile_edge), probe_total)


MESH = pl.DeviceIdType.MESH
VM = pltpu.VMEM
SM = pltpu.SMEM


def one_hot(rows, cols, shift):
    row = lax.broadcasted_iota(jnp.int32, (rows, cols), 0)
    col = lax.broadcasted_iota(jnp.int32, (rows, cols), 1)
    return jnp.where(col == row + shift, 1.0, 0.0).astype(jnp.bfloat16)


def bdot(a, b):
    return jnp.dot(a, b, preferred_element_type=jnp.float32)


def class_of(tmap, me, per):
    found = jnp.int32(0)
    for r in range(OWN_R):
        found = jnp.where(lax.div(tmap[r, 0], per) == me, r, found)
    return found


def place(off, n, rho):
    y = off[n, 0]
    x = off[n, 1]
    ty = lax.div(y, TS)
    tx = lax.div(x, TS)
    step = lax.rem(rho - ty + 64 * OWN_R, OWN_R)
    return ty + step, tx, x - tx * TS, step < 3


def pack_kernel(owners, layers, per, off, tmap, tiles, slots):
    me = lax.axis_index("pos")
    z = lax.axis_index("tile")
    rho = class_of(tmap, me, per)
    for p in range(owners):
        row, tx, ix, live = place(off, p * layers + z, rho)

        @pl.when(live)
        def _():
            acc = None
            for j in range(3):
                local = tmap[row, tx + j] - me * per
                part = bdot(tiles[local], one_hot(TS, 2 * TS, TS * j - ix))
                acc = part if acc is None else acc + part
            slots[p] = acc.astype(jnp.bfloat16)


def fetch_kernel(owners, slots, got, send_sem, recv_sem, own_sem):
    me = lax.axis_index("pos")
    z = lax.axis_index("tile")
    barrier = pltpu.get_barrier_semaphore()
    for d in range(1, owners):
        peer = lax.rem(me + d, owners)
        pl.semaphore_signal(barrier, inc=1, device_id=(peer, z), device_id_type=MESH)
    own = pltpu.make_async_copy(slots.at[me], got.at[me], own_sem)
    own.start()
    pl.semaphore_wait(barrier, owners - 1)
    copies = []
    for d in range(1, owners):
        peer = lax.rem(me + d, owners)
        copy = pltpu.make_async_remote_copy(
            src_ref=slots.at[peer],
            dst_ref=got.at[me],
            send_sem=send_sem.at[d],
            recv_sem=recv_sem.at[d],
            device_id=(peer, z),
            device_id_type=MESH,
        )
        copy.start()
        copies.append(copy)
    own.wait()
    for copy in copies:
        copy.wait()


def split(a):
    high = a.astype(jnp.bfloat16)
    return high, (a - high.astype(jnp.float32)).astype(jnp.bfloat16)


def rmul(a, table):
    high, low = split(a)
    return bdot(high, table[0]) + (bdot(low, table[0]) + bdot(high, table[1]))


def lmul(table, a):
    high, low = split(a)
    return bdot(table[0], high) + (bdot(table[0], low) + bdot(table[1], high))


def both_sides(re, im, right, left):
    width = re.shape[1]
    mid = rmul(jnp.concatenate([re, im], axis=1), right)
    out = lmul(left, jnp.concatenate([mid[:, :width], mid[:, width:]], axis=0))
    return out[:width], out[width:]


def wave_kernel(layers, per, off, tmap, got, probe, intens, tables, patch_out, pgrad):
    n = lax.axis_index("pos") * layers + lax.axis_index("tile")
    y = off[n, 0]
    ty = lax.div(y, TS)
    iy = y - ty * TS
    w = probe.shape[-1]
    owner = [lax.div(tmap[ty + s, 0], per) for s in range(3)]
    rows = []
    for s in range(3):
        block = got[owner[s]]
        rows.append(jnp.concatenate([block[k * TS : (k + 1) * TS] for k in range(4)], axis=1))
    patch = bdot(one_hot(w, 3 * TS, iy), jnp.concatenate(rows, axis=0))
    en_re, en_im, ex_re, ex_im = (patch[:, k * w : (k + 1) * w] for k in range(4))
    pr, pi = probe[0], probe[1]
    fw, fc, aw, ac = ((tables[2 * i], tables[2 * i + 1]) for i in range(4))
    re, im = product(pr, pi, en_re, en_im)
    sp_re, sp_im = both_sides(re, im, aw, ac)
    re, im = product(sp_re, sp_im, ex_re, ex_im)
    far_re, far_im = both_sides(re, im, fw, fc)
    excess = far_re * far_re + far_im * far_im - intens[0]
    bk_re, bk_im = both_sides(excess * far_re, excess * far_im, fc, fw)
    gx_re, gx_im = product(sp_re, -sp_im, bk_re, bk_im)
    re, im = product(ex_re, -ex_im, bk_re, bk_im)
    in_re, in_im = both_sides(re, im, ac, aw)
    ge_re, ge_im = product(pr, -pi, in_re, in_im)
    gp_re, gp_im = product(en_re, -en_im, in_re, in_im)
    pgrad[0:w] = gp_re
    pgrad[w : 2 * w] = gp_im
    for k, part in enumerate((ge_re, ge_im, gx_re, gx_im)):
        patch_out[k // 2, (k % 2) * w : (k % 2 + 1) * w, :] = part.astype(jnp.bfloat16)


def spread_kernel(
    owners, layers, patch, pgrad, got, ptotal, part, summed, layer_part,
    own_sem, l_send, l_recv, z_send, z_recv, c_send, c_recv,
    p_send, p_recv, q_send, q_recv, r_send, r_recv,
):
    me = lax.axis_index("pos")
    z = lax.axis_index("tile")
    core = lax.rem(me, 2)
    x = lax.rem(lax.div(me, 2), 2)
    y = lax.div(me, 4)
    mates = [4 * b + 2 * a for b in (y, 1 - y) for a in (x, 1 - x)]
    same = [m + core for m in mates]
    other = [m + 1 - core for m in mates]
    chunk = pgrad.shape[0] // owners
    half = patch.shape[1] // 2

    def remote(src, dst, ssem, rsem, p, t):
        return pltpu.make_async_remote_copy(
            src_ref=src, dst_ref=dst, send_sem=ssem, recv_sem=rsem,
            device_id=(p, t), device_id_type=MESH,
        )

    barrier = pltpu.get_barrier_semaphore()
    for d in range(1, owners):
        pl.semaphore_signal(
            barrier, inc=1, device_id=(lax.rem(me + d, owners), z), device_id_type=MESH
        )
    for d in range(1, layers):
        pl.semaphore_signal(
            barrier, inc=1, device_id=(me, lax.rem(z + d, layers)), device_id_type=MESH
        )
    own = pltpu.make_async_copy(patch, got.at[:, z, me], own_sem)
    own.start()
    pl.semaphore_wait(barrier, owners + layers - 2)

    def item(h, t, p, rows=None):
        ref = got.at[h, t, p]
        return ref if rows is None else ref.at[pl.ds(rows * half, half)]

    def across(h, t, i):
        return remote(
            item(h, t, me), item(h, t, me), l_send.at[h, t, i], l_recv.at[h, t, i], same[i], z
        )

    def arrived(h, t, i):
        return remote(
            item(h, t, same[i]), item(h, t, same[i]),
            l_send.at[h, t, i], l_recv.at[h, t, i], same[i], z,
        )

    def corner(h, t, r, came, to):
        ref = item(h, t, same[came], r)
        k = 0 if r == 0 else 3
        return remote(ref, ref, l_send.at[h, t, k], l_recv.at[h, t, k], same[to], z)

    def corner_in(h, t, r):
        ref = item(h, t, same[3], r)
        k = 0 if r == 0 else 3
        return remote(ref, ref, l_send.at[h, t, k], l_recv.at[h, t, k], same[3], z)

    def hand(h, t, i):
        ref = item(h, t, same[i])
        return remote(ref, ref, c_send.at[h, t, i], c_recv.at[h, t, i], other[0], z)

    def handed(h, t, i):
        ref = item(h, t, other[i])
        return remote(ref, ref, c_send.at[h, t, i], c_recv.at[h, t, i], other[0], z)

    def climb(h, way, t, i, layer, target):
        ref = item(h, layer, same[i])
        return remote(ref, ref, z_send.at[h, way, t, i], z_recv.at[h, way, t, i], me, target)

    def leave(h, i):
        @pl.when(z < layers - 1)
        def _():
            climb(h, 0, 0, i, z, z + 1).start()

        @pl.when(z > 0)
        def _():
            climb(h, 1, 0, i, z, z - 1).start()

    probes = []
    for d in range(1, owners):
        peer = lax.rem(me + d, owners)
        probes.append(
            remote(
                pgrad.at[pl.ds(pl.multiple_of(peer * chunk, chunk), chunk)],
                part.at[me], p_send.at[d], p_recv.at[d], peer, z,
            )
        )
        probes[-1].start()
    own.wait()
    across(0, z, 1).start()
    across(0, z, 2).start()
    leave(1, 0)
    leave(0, 0)
    across(1, z, 1).start()
    across(1, z, 2).start()
    hand(0, z, 0).start()
    hand(1, z, 0).start()

    part[me] = pgrad[pl.ds(pl.multiple_of(me * chunk, chunk), chunk)]
    for copy in probes:
        copy.wait()
    summed[...] = jnp.sum(part[...], axis=0)
    layer_part[z] = summed[...]
    zs = []
    for d in range(1, layers):
        zs.append(
            remote(
                summed, layer_part.at[z], q_send.at[d], q_recv.at[d],
                me, lax.rem(z + d, layers),
            )
        )
        zs[-1].start()

    def sides(h, t):
        arrived(h, t, 1).wait_recv()
        corner(h, t, 0, 1, 2).start()
        hand(h, t, 1).start()
        if h == 0:
            leave(0, 1)
        arrived(h, t, 2).wait_recv()
        corner(h, t, 1, 2, 1).start()
        hand(h, t, 2).start()
        if h == 0:
            leave(0, 2)

    def last(h, t):
        corner_in(h, t, 0).wait_recv()
        corner_in(h, t, 1).wait_recv()
        hand(h, t, 3).start()
        if h == 0:
            leave(0, 3)

    def step_z(h, t, i):
        for way, layer, there in ((0, z - 1 - t, z + 1), (1, z + 1 + t, z - 1)):
            @pl.when((layer >= 0) & (layer <= layers - 1))
            def _():
                climb(h, way, t, i, layer, there).wait_recv()
                if t < layers - 2:

                    @pl.when((there >= 0) & (there <= layers - 1))
                    def _():
                        climb(h, way, t + 1, i, layer, there).start()

                hand(h, layer, i).start()
                if h == 1:
                    across(1, layer, 1).start()
                    across(1, layer, 2).start()

    sides(0, z)
    step_z(1, 0, 0)
    last(0, z)
    for copy in zs:
        copy.wait()
    ptotal[me] = jnp.sum(layer_part[...], axis=0)
    outs = []
    for d in range(1, owners):
        outs.append(
            remote(
                ptotal.at[me], ptotal.at[me], r_send.at[d], r_recv.at[d],
                lax.rem(me + d, owners), z,
            )
        )
        outs[-1].start()
    sides(1, z)
    for t in range(layers - 1):
        if t > 0:
            step_z(1, t, 0)
        for i in range(4):
            step_z(0, t, i)
        if t == 0:
            last(1, z)
        for layer in (z - 1 - t, z + 1 + t):
            @pl.when((layer >= 0) & (layer <= layers - 1))
            def _():
                sides(1, layer)
                last(1, layer)

    for copy in outs:
        copy.wait()

    @pl.loop(0, layers)
    def _(t):
        for h in range(2):
            for i in range(4):
                hand(h, t, i).wait_send()
                handed(h, t, i).wait_recv()

    def drained(h, t):
        across(h, t, 1).wait_send()
        across(h, t, 2).wait_send()
        corner(h, t, 0, 1, 2).wait_send()
        corner(h, t, 1, 2, 1).wait_send()

    drained(0, z)

    @pl.loop(0, layers)
    def _(t):
        drained(1, t)

    for t in range(layers - 1):
        for way, layer, there in ((0, z - t, z + 1), (1, z + t, z - 1)):
            @pl.when(
                (layer >= 0) & (layer <= layers - 1) & (there >= 0) & (there <= layers - 1)
            )
            def _():
                climb(1, way, t, 0, layer, there).wait_send()
                for i in range(4):
                    climb(0, way, t, i, layer, there).wait_send()


def add_kernel(owners, layers, per, off, tmap, got, out):
    me = lax.axis_index("pos")
    rho = class_of(tmap, me, per)
    out[...] = jnp.zeros_like(out)

    @pl.loop(0, owners * layers)
    def _(n):
        row, tx, ix, live = place(off, n, rho)

        @pl.when(live)
        def _():
            w = 2 * TS
            pick_rows = one_hot(TS, w, row * TS - off[n, 0])
            t, p = lax.rem(n, layers), lax.div(n, layers)
            first, second = got[0, t, p], got[1, t, p]
            wide = jnp.concatenate([first[:w], first[w:], second[:w], second[w:]], axis=1)
            rows = bdot(pick_rows, wide).astype(jnp.bfloat16)
            block = jnp.concatenate([rows[:, k * w : (k + 1) * w] for k in range(4)], axis=0)
            for j in range(3):
                local = tmap[row, tx + j] - me * per
                out[local] += bdot(block, one_hot(w, TS, ix - TS * j))


def spectral_blocks(width):
    k = np.arange(width)
    fwd = np.exp(-2j * np.pi * (np.outer(k, k) % width) / width) / np.sqrt(width)
    centred = (k + width // 2) % width - width // 2
    phase = np.exp(-0.2j * centred * centred / width)
    ahead = np.conj(fwd) @ (phase[:, None] * fwd)
    found = []
    for m in (fwd, np.conj(fwd), ahead, np.conj(ahead)):
        full = np.block([[m.real, m.imag], [-m.imag, m.real]]).astype(np.float32)
        high = full.astype(jnp.bfloat16)
        found += [high, (full - high.astype(np.float32)).astype(jnp.bfloat16)]
    return np.stack(found)


def params(**kw):
    return pltpu.CompilerParams(vmem_limit_bytes=32 * 1024 * 1024, **kw)


def row_plan(obj_tiles, tile_map, offsets, probe, intens):
    owners = lax.axis_size("pos")
    layers = lax.axis_size("tile")
    per = obj_tiles.shape[0]
    w = probe.shape[-1]
    bf, f32 = jnp.bfloat16, jnp.float32
    vm = pl.BlockSpec(memory_space=VM)
    sm = pl.BlockSpec(memory_space=SM)
    dma = pltpu.SemaphoreType.DMA
    tiles = obj_tiles.reshape(per, 4 * TS, TS)
    slot_shape = jax.ShapeDtypeStruct((owners, 4 * TS, w), bf)
    slots = pl.pallas_call(
        functools.partial(pack_kernel, owners, layers, per),
        out_shape=slot_shape,
        in_specs=[sm, sm, vm],
        out_specs=vm,
        compiler_params=params(),
    )(offsets, tile_map, tiles)
    got = pl.pallas_call(
        functools.partial(fetch_kernel, owners),
        out_shape=slot_shape,
        in_specs=[vm],
        out_specs=vm,
        scratch_shapes=[dma((owners,)), dma((owners,)), dma],
        compiler_params=params(collective_id=0, has_side_effects=True),
    )(slots)
    tables = jnp.asarray(spectral_blocks(w))
    grads, pgrad = pl.pallas_call(
        functools.partial(wave_kernel, layers, per),
        out_shape=[
            jax.ShapeDtypeStruct((2, 2 * w, w), bf),
            jax.ShapeDtypeStruct((2 * w, w), f32),
        ],
        in_specs=[sm, sm, vm, vm, vm, vm],
        out_specs=[vm, vm],
        compiler_params=params(),
    )(offsets, tile_map, got, probe, intens, tables)
    chunk = 2 * w // owners
    spread, ptotal = pl.pallas_call(
        functools.partial(spread_kernel, owners, layers),
        out_shape=[
            jax.ShapeDtypeStruct((2, layers, owners, 2 * w, w), bf),
            jax.ShapeDtypeStruct((owners, chunk, w), f32),
        ],
        in_specs=[vm, vm],
        out_specs=[vm, vm],
        scratch_shapes=[
            VM((owners, chunk, w), f32), VM((chunk, w), f32), VM((layers, chunk, w), f32), dma,
            dma((2, layers, 4)), dma((2, layers, 4)),
            dma((2, 2, layers, 4)), dma((2, 2, layers, 4)),
            dma((2, layers, 4)), dma((2, layers, 4)),
            dma((owners,)), dma((owners,)), dma((layers,)), dma((layers,)), dma((owners,)), dma((owners,)),
        ],
        compiler_params=params(collective_id=1, has_side_effects=True),
    )(grads, pgrad)
    total = pl.pallas_call(
        functools.partial(add_kernel, owners, layers, per),
        out_shape=jax.ShapeDtypeStruct((per, 4 * TS, TS), f32),
        in_specs=[sm, sm, vm],
        out_specs=vm,
        compiler_params=params(),
    )(offsets, tile_map, spread)
    return (total.reshape(per, 4, TS * TS), ptotal.reshape(2, w, w))


def solution(mesh):
    in_specs = (P("pos", None, None), P(), P(), P(), P(("pos", "tile"), None, None))
    out_specs = (P("pos", None, None), P())
    plan = row_plan if mesh.shape["pos"] == OWN_R else general_plan
    return jax.shard_map(plan, mesh=mesh, in_specs=in_specs, out_specs=out_specs, check_vma=False)
```

```python
import functools
import math

import jax
import jax.numpy as jnp
import numpy as np
from jax import lax
from jax.experimental import pallas as pl
from jax.experimental.pallas import tpu as pltpu
from jax.sharding import PartitionSpec as P

TS = 64
OWN_R = 8


def matmul_hi(left_op, right_op):
    return jnp.dot(
        left_op, right_op, precision=lax.Precision.HIGHEST, preferred_element_type=jnp.float32
    )


def spectral_tables(width_px):
    positions = jnp.arange(width_px, dtype=jnp.int32)
    phase_idx = positions[:, None] * positions[None, :] % width_px
    angles = phase_idx.astype(jnp.float32) * (2.0 * math.pi / width_px)
    norm_factor = 1.0 / math.sqrt(width_px)
    return (jnp.cos(angles) * norm_factor, -jnp.sin(angles) * norm_factor)


def complex_matmul(left_re, left_im, right_re, right_im):
    out_re = matmul_hi(left_re, right_re) - matmul_hi(left_im, right_im)
    out_im = matmul_hi(left_re, right_im) + matmul_hi(left_im, right_re)
    return (out_re, out_im)


def propagation_matrix(width_px, fwd_re, fwd_im, sign_val):
    positions = jnp.arange(width_px, dtype=jnp.int32)
    centred = (positions + width_px // 2) % width_px - width_px // 2
    angles = (centred * centred).astype(jnp.float32) * (-0.2 / width_px) * sign_val
    phase_re = jnp.cos(angles)[:, None]
    phase_im = jnp.sin(angles)[:, None]
    scaled_re = phase_re * fwd_re - phase_im * fwd_im
    scaled_im = phase_re * fwd_im + phase_im * fwd_re
    return complex_matmul(fwd_re, -fwd_im, scaled_re, scaled_im)


def transform(part_re, part_im, table_re, table_im):
    mid_re, mid_im = complex_matmul(part_re, part_im, table_re, table_im)
    return complex_matmul(table_re, table_im, mid_re, mid_im)


def product(left_re, left_im, right_re, right_im):
    return (left_re * right_re - left_im * right_im, left_re * right_im + left_im * right_re)


def pick(table, ids):
    rows = jnp.arange(table.shape[0], dtype=jnp.int32)
    chooser = (ids.reshape(-1)[:, None] == rows[None, :]).astype(table.dtype)
    flat = jnp.dot(
        chooser, table.reshape(table.shape[0], -1), preferred_element_type=jnp.float32
    ).astype(table.dtype)
    return flat.reshape(ids.shape + table.shape[1:])


def general_plan(obj_tiles, tile_map, offsets, probe, intens):
    owners = lax.axis_size("pos")
    layers = lax.axis_size("tile")
    me_pos = lax.axis_index("pos")
    me_tile = lax.axis_index("tile")
    tiles_dev = obj_tiles.shape[0]
    tile_edge = TS
    width_px = probe.shape[-1]
    tile_span = width_px // tile_edge + 1
    cols_own = owners // OWN_R
    cols_cap = (tile_span + cols_own - 1) // cols_own
    slots = (tile_span + OWN_R - 1) // OWN_R * cols_cap
    span_idx = jnp.arange(tile_span, dtype=jnp.int32)
    slot_grid = (span_idx[:, None] // OWN_R * cols_cap + span_idx[None, :] // cols_own).reshape(-1)

    def footprint(corner):
        row_ids = corner[0] // tile_edge + span_idx
        col_ids = corner[1] // tile_edge + span_idx
        store_id = tile_map[row_ids[:, None], col_ids[None, :]].reshape(-1)
        owner_id = store_id // tiles_dev
        return (owner_id, store_id - owner_id * tiles_dev)

    by_device = offsets.reshape(owners, layers, 2)
    peer_corners = lax.dynamic_index_in_dim(by_device, me_tile, 1, keepdims=False)
    peer_owner, peer_local = jax.vmap(footprint)(peer_corners)
    slot_ids = jnp.arange(slots, dtype=jnp.int32)
    matches = (peer_owner == me_pos)[:, :, None] & (
        slot_grid[None, :, None] == slot_ids[None, None, :]
    )
    send_local = jnp.sum(jnp.where(matches, peer_local[:, :, None], 0), axis=1)
    send_live = jnp.any(matches, axis=1)
    chosen = jnp.where(
        send_live[:, :, None, None], pick(obj_tiles, send_local), jnp.zeros((), obj_tiles.dtype)
    )
    my_corner = lax.dynamic_index_in_dim(offsets, me_pos * layers + me_tile, 0, keepdims=False)
    my_owner, my_local = footprint(my_corner)
    flat_slot = my_owner * slots + slot_grid
    inner_y = my_corner[0] % tile_edge
    inner_x = my_corner[1] % tile_edge
    zero_idx = jnp.zeros((), jnp.int32)
    fwd_re, fwd_im = spectral_tables(width_px)
    ahead_re, ahead_im = propagation_matrix(width_px, fwd_re, fwd_im, 1.0)
    behind_re, behind_im = propagation_matrix(width_px, fwd_re, fwd_im, -1.0)
    probe_re = probe[0]
    probe_im = probe[1]
    received = lax.all_to_all(chosen, "pos", split_axis=0, concat_axis=0, tiled=True)
    n_comps = received.shape[2]
    pieces = pick(
        received.reshape(owners * slots, n_comps, tile_edge * tile_edge), flat_slot
    )
    region = pieces.reshape(tile_span, tile_span, n_comps, tile_edge, tile_edge).transpose(
        2, 0, 3, 1, 4
    )
    region = region.reshape(n_comps, tile_span * tile_edge, tile_span * tile_edge)
    patch_px = lax.dynamic_slice(
        region, (zero_idx, inner_y, inner_x), (n_comps, width_px, width_px)
    )
    fetched = patch_px.astype(jnp.float32)
    entry_patch = fetched[:2]
    leaving = fetched[2:]
    first_re, first_im = product(probe_re, probe_im, entry_patch[0], entry_patch[1])
    spread_re, spread_im = transform(first_re, first_im, ahead_re, ahead_im)
    second_re, second_im = product(spread_re, spread_im, leaving[0], leaving[1])
    far_re, far_im = transform(second_re, second_im, fwd_re, fwd_im)
    excess = far_re * far_re + far_im * far_im - intens[0]
    back_re, back_im = transform(excess * far_re, excess * far_im, fwd_re, -fwd_im)
    exit_re, exit_im = product(spread_re, -spread_im, back_re, back_im)
    mid_re, mid_im = product(leaving[0], -leaving[1], back_re, back_im)
    inner_re, inner_im = transform(mid_re, mid_im, behind_re, behind_im)
    entry_re, entry_im = product(probe_re, -probe_im, inner_re, inner_im)
    grad_re, grad_im = product(entry_patch[0], -entry_patch[1], inner_re, inner_im)
    patch_grad = jnp.stack([entry_re, entry_im, exit_re, exit_im]).astype(jnp.bfloat16)
    region = jnp.zeros((4, tile_span * tile_edge, tile_span * tile_edge), jnp.bfloat16)
    region = lax.dynamic_update_slice(region, patch_grad, (zero_idx, inner_y, inner_x))
    pieces = region.reshape(4, tile_span, tile_edge, tile_span, tile_edge).transpose(1, 3, 0, 2, 4)
    pieces = pieces.reshape(tile_span * tile_span, 4, tile_edge * tile_edge)
    outgoing = (
        jnp.zeros((owners * slots, 4, tile_edge * tile_edge), jnp.bfloat16)
        .at[flat_slot]
        .set(pieces)
    )
    outgoing = outgoing.reshape(owners, slots, 4, tile_edge * tile_edge)
    returned = lax.all_to_all(outgoing, "pos", split_axis=0, concat_axis=0, tiled=True)
    tile_ids = jnp.arange(tiles_dev, dtype=jnp.int32)
    selector = (
        (send_local.reshape(-1)[None, :] == tile_ids[:, None]) & send_live.reshape(-1)[None, :]
    ).astype(jnp.bfloat16)
    local_sum = jnp.dot(
        selector,
        returned.reshape(owners * slots, 4 * tile_edge * tile_edge),
        preferred_element_type=jnp.float32,
    )
    probe_part = jnp.stack([grad_re, grad_im])
    tile_total, probe_layer = lax.psum((local_sum, probe_part), "tile")
    probe_total = lax.psum(probe_layer, "pos")
    return (tile_total.reshape(tiles_dev, 4, tile_edge * tile_edge), probe_total)


MESH = pl.DeviceIdType.MESH
VM = pltpu.VMEM
SM = pltpu.SMEM


HALF = TS // 2


def indices(rows, cols):
    return (
        lax.broadcasted_iota(jnp.int32, (rows, cols), 0),
        lax.broadcasted_iota(jnp.int32, (rows, cols), 1),
    )


def ones_at(where):
    return jnp.where(where, 1.0, 0.0).astype(jnp.bfloat16)


def stored_row(index):
    return 2 * lax.rem(index, HALF) + lax.div(index, HALF)


def bdot(a, b):
    return jnp.dot(a, b, preferred_element_type=jnp.float32)


class Maps:
    def __init__(self, offsets, tile_map):
        self.offsets, self.tile_map = offsets, tile_map

    def corner(self, n):
        return self.offsets[0, n], self.offsets[1, n]

    def tile(self, row, col):
        return self.tile_map[col, row]

    def class_of(self, me, per):
        found = jnp.int32(0)
        for r in range(OWN_R):
            found = jnp.where(lax.div(self.tile(r, 0), per) == me, r, found)
        return found

    def place(self, n, rho):
        y, x = self.corner(n)
        ty = lax.div(y, TS)
        tx = lax.div(x, TS)
        step = lax.rem(rho - ty + 64 * OWN_R, OWN_R)
        return ty + step, tx, x - tx * TS, step < 3


def crop(maps, n, rho, me, per, rows, tiles):
    row, tx, ix, _ = maps.place(n, rho)
    row = jnp.minimum(row, rows - 1)
    r, c = indices(2 * TS, 4 * TS)
    same_parity = lax.div(r, TS) == lax.div(c, 2 * TS)
    px, q = lax.rem(r, TS), lax.rem(c, 2 * TS)
    acc = None
    for j in range(3):
        local = jnp.clip(maps.tile(row, tx + j) - me * per, 0, per - 1)
        part = bdot(tiles[local], ones_at(same_parity & (q == px + (TS * j - ix))))
        acc = part if acc is None else acc + part
    return acc.astype(jnp.bfloat16)


def split(a):
    high = a.astype(jnp.bfloat16)
    return high, (a - high.astype(jnp.float32)).astype(jnp.bfloat16)


def rmul(a, table):
    high, low = split(a)
    return bdot(high, table[0]) + (bdot(low, table[0]) + bdot(high, table[1]))


def lmul(table, a):
    high, low = split(a)
    return bdot(table[0], high) + (bdot(table[0], low) + bdot(table[1], high))


def both_sides(re, im, right, left):
    width = re.shape[1]
    mid = rmul(jnp.concatenate([re, im], axis=1), right)
    out = lmul(left, jnp.concatenate([mid[:, :width], mid[:, width:]], axis=0))
    return out[:width], out[width:]


def wave(maps, n, per, got, probe, intens, tables, keep, exit_done):
    y, _ = maps.corner(n)
    ty = lax.div(y, TS)
    iy = y - ty * TS
    w = probe.shape[-1]
    rows = []
    for s in range(3):
        block = got[lax.div(maps.tile(ty + s, 0), per)]
        for half in (block[:, :w], block[:, w:]):
            rows.append(jnp.concatenate([half[k * HALF : (k + 1) * HALF] for k in range(4)], axis=1))
    r, c = indices(w, 3 * TS)
    picks = ones_at(r + iy == lax.div(c, TS) * TS + stored_row(lax.rem(c, TS)))
    patch = bdot(picks, jnp.concatenate(rows, axis=0))
    en_re, en_im, ex_re, ex_im = (patch[:, k * w : (k + 1) * w] for k in range(4))
    pr, pi = probe[0], probe[1]
    fw, fc, aw, ac = ((tables[2 * i], tables[2 * i + 1]) for i in range(4))
    re, im = product(pr, pi, en_re, en_im)
    sp_re, sp_im = both_sides(re, im, aw, ac)
    re, im = product(sp_re, sp_im, ex_re, ex_im)
    far_re, far_im = both_sides(re, im, fw, fc)
    excess = far_re * far_re + far_im * far_im - intens[0]
    bk_re, bk_im = both_sides(excess * far_re, excess * far_im, fc, fw)
    keep(1, *product(sp_re, -sp_im, bk_re, bk_im))
    exit_done()
    re, im = product(ex_re, -ex_im, bk_re, bk_im)
    in_re, in_im = both_sides(re, im, ac, aw)
    keep(0, *product(pr, -pi, in_re, in_im))
    return product(en_re, -en_im, in_re, in_im)


def main_kernel(
    owners, layers, per, rows, offsets, tile_map, tiles, probe, intens, tables, got, ptotal,
    slots, fetched, pgrad, part, summed, layer_part,
    f_send, f_recv, l_send, l_recv, z_send, z_recv, c_send, c_recv,
    p_send, p_recv, q_send, q_recv, r_send, r_recv,
):
    me = lax.axis_index("pos")
    z = lax.axis_index("tile")
    core = lax.rem(me, 2)
    x = lax.rem(lax.div(me, 2), 2)
    y = lax.div(me, 4)
    mates = [4 * b + 2 * a for b in (y, 1 - y) for a in (x, 1 - x)]
    same = [m + core for m in mates]
    other = [m + 1 - core for m in mates]
    chunk = pgrad.shape[0] // owners
    w = probe.shape[-1]
    half = w
    maps = Maps(offsets, tile_map)

    def remote(src, dst, ssem, rsem, p, t):
        return pltpu.make_async_remote_copy(
            src_ref=src, dst_ref=dst, send_sem=ssem, recv_sem=rsem,
            device_id=(p, t), device_id_type=MESH,
        )

    barrier = pltpu.get_barrier_semaphore()
    for d in range(1, owners):
        pl.semaphore_signal(
            barrier, inc=1, device_id=(lax.rem(me + d, owners), z), device_id_type=MESH
        )
    for d in range(1, layers):
        pl.semaphore_signal(
            barrier, inc=1, device_id=(me, lax.rem(z + d, layers)), device_id_type=MESH
        )
    rho = maps.class_of(me, per)
    fetches = []
    for d in range(1, owners):
        peer = lax.rem(me + d, owners)
        slots[d] = crop(maps, peer * layers + z, rho, me, per, rows, tiles)
        if d == 1:
            pl.semaphore_wait(barrier, owners + layers - 2)
        fetches.append(remote(slots.at[d], fetched.at[me], f_send.at[d], f_recv.at[d], peer, z))
        fetches[-1].start()
    fetched[me] = crop(maps, me * layers + z, rho, me, per, rows, tiles)

    def item(h, t, p, rows=None):
        ref = got.at[h, t, p]
        return ref if rows is None else ref.at[pl.ds(rows * half, half)]

    def across(h, t, i):
        return remote(
            item(h, t, me), item(h, t, me), l_send.at[h, t, i], l_recv.at[h, t, i], same[i], z
        )

    def arrived(h, t, i):
        return remote(
            item(h, t, same[i]), item(h, t, same[i]),
            l_send.at[h, t, i], l_recv.at[h, t, i], same[i], z,
        )

    def corner(h, t, r, came, to):
        ref = item(h, t, same[came], r)
        k = 0 if r == 0 else 3
        return remote(ref, ref, l_send.at[h, t, k], l_recv.at[h, t, k], same[to], z)

    def corner_in(h, t, r):
        ref = item(h, t, same[3], r)
        k = 0 if r == 0 else 3
        return remote(ref, ref, l_send.at[h, t, k], l_recv.at[h, t, k], same[3], z)

    def hand(h, t, i):
        ref = item(h, t, same[i])
        return remote(ref, ref, c_send.at[h, t, i], c_recv.at[h, t, i], other[0], z)

    def handed(h, t, i):
        ref = item(h, t, other[i])
        return remote(ref, ref, c_send.at[h, t, i], c_recv.at[h, t, i], other[0], z)

    def climb(h, way, t, i, layer, target):
        ref = item(h, layer, same[i])
        return remote(ref, ref, z_send.at[h, way, t, i], z_recv.at[h, way, t, i], me, target)

    def leave(h, i):
        @pl.when(z < layers - 1)
        def _():
            climb(h, 0, 0, i, z, z + 1).start()

        @pl.when(z > 0)
        def _():
            climb(h, 1, 0, i, z, z - 1).start()

    def sides(h, t):
        arrived(h, t, 1).wait_recv()
        corner(h, t, 0, 1, 2).start()
        hand(h, t, 1).start()
        if h == 0:
            leave(0, 1)
        arrived(h, t, 2).wait_recv()
        corner(h, t, 1, 2, 1).start()
        hand(h, t, 2).start()
        if h == 0:
            leave(0, 2)

    def last(h, t):
        corner_in(h, t, 0).wait_recv()
        corner_in(h, t, 1).wait_recv()
        hand(h, t, 3).start()
        if h == 0:
            leave(0, 3)

    def step_z(h, t, i):
        for way, layer, there in ((0, z - 1 - t, z + 1), (1, z + 1 + t, z - 1)):
            @pl.when((layer >= 0) & (layer <= layers - 1))
            def _():
                climb(h, way, t, i, layer, there).wait_recv()
                if t < layers - 2:

                    @pl.when((there >= 0) & (there <= layers - 1))
                    def _():
                        climb(h, way, t + 1, i, layer, there).start()

                hand(h, layer, i).start()
                if h == 1:
                    across(1, layer, 1).start()
                    across(1, layer, 2).start()

    def keep(h, re, im):
        got[h, z, me, 0:w] = re.astype(jnp.bfloat16)
        got[h, z, me, w : 2 * w] = im.astype(jnp.bfloat16)

    def exit_done():
        leave(1, 0)
        across(1, z, 1).start()
        across(1, z, 2).start()
        hand(1, z, 0).start()

    for copy in fetches:
        copy.wait_recv()
    gp_re, gp_im = wave(
        maps, me * layers + z, per, fetched, probe, intens, tables, keep, exit_done
    )
    across(0, z, 1).start()
    across(0, z, 2).start()
    leave(0, 0)
    hand(0, z, 0).start()
    pgrad[0:w] = gp_re
    pgrad[w : 2 * w] = gp_im
    probes = []
    for d in range(1, owners):
        peer = lax.rem(me + d, owners)
        probes.append(
            remote(
                pgrad.at[pl.ds(pl.multiple_of(peer * chunk, chunk), chunk)],
                part.at[me], p_send.at[d], p_recv.at[d], peer, z,
            )
        )
        probes[-1].start()
    sides(0, z)
    step_z(1, 0, 0)
    part[me] = pgrad[pl.ds(pl.multiple_of(me * chunk, chunk), chunk)]
    for copy in probes:
        copy.wait()
    summed[...] = jnp.sum(part[...], axis=0)
    layer_part[z] = summed[...]
    zs = []
    for d in range(1, layers):
        zs.append(
            remote(
                summed, layer_part.at[z], q_send.at[d], q_recv.at[d],
                me, lax.rem(z + d, layers),
            )
        )
        zs[-1].start()

    last(0, z)
    for copy in zs:
        copy.wait()
    ptotal[me] = jnp.sum(layer_part[...], axis=0)
    outs = []
    for d in range(1, owners):
        outs.append(
            remote(
                ptotal.at[me], ptotal.at[me], r_send.at[d], r_recv.at[d],
                lax.rem(me + d, owners), z,
            )
        )
        outs[-1].start()
    sides(1, z)
    for t in range(layers - 1):
        if t > 0:
            step_z(1, t, 0)
        for i in range(4):
            step_z(0, t, i)
        if t == 0:
            last(1, z)
        for layer in (z - 1 - t, z + 1 + t):
            @pl.when((layer >= 0) & (layer <= layers - 1))
            def _():
                sides(1, layer)
                last(1, layer)

    for copy in outs:
        copy.wait()
    for copy in fetches:
        copy.wait_send()

    @pl.loop(0, layers)
    def _(t):
        for h in range(2):
            for i in range(4):
                hand(h, t, i).wait_send()
                handed(h, t, i).wait_recv()

    def drained(h, t):
        across(h, t, 1).wait_send()
        across(h, t, 2).wait_send()
        corner(h, t, 0, 1, 2).wait_send()
        corner(h, t, 1, 2, 1).wait_send()

    drained(0, z)

    @pl.loop(0, layers)
    def _(t):
        drained(1, t)

    for t in range(layers - 1):
        for way, layer, there in ((0, z - t, z + 1), (1, z + t, z - 1)):
            @pl.when(
                (layer >= 0) & (layer <= layers - 1) & (there >= 0) & (there <= layers - 1)
            )
            def _():
                climb(1, way, t, 0, layer, there).wait_send()
                for i in range(4):
                    climb(0, way, t, i, layer, there).wait_send()


def add_kernel(owners, layers, per, offsets, tile_map, got, out):
    me = lax.axis_index("pos")
    maps = Maps(offsets, tile_map)
    rho = maps.class_of(me, per)
    w = 2 * TS
    out[...] = jnp.zeros_like(out)

    @pl.loop(0, owners * layers)
    def _(n):
        row, tx, ix, live = maps.place(n, rho)

        @pl.when(live)
        def _():
            r, c = indices(TS, w)
            picks = ones_at(c == stored_row(r) + (row * TS - maps.corner(n)[0]))
            t, p = lax.rem(n, layers), lax.div(n, layers)
            first, second = got[0, t, p], got[1, t, p]
            wide = jnp.concatenate([first[:w], first[w:], second[:w], second[w:]], axis=1)
            rows = bdot(picks, wide).astype(jnp.bfloat16)
            block = jnp.concatenate(
                [
                    jnp.concatenate(
                        [rows[:HALF, k * w : (k + 1) * w], rows[HALF:, k * w : (k + 1) * w]], axis=1
                    )
                    for k in range(4)
                ],
                axis=0,
            )
            r, c = indices(2 * w, w)
            same_parity = lax.div(r, w) == lax.div(c, TS)
            q, px = lax.rem(r, w), lax.rem(c, TS)
            for j in range(3):
                local = maps.tile(row, tx + j) - me * per
                out[local] += bdot(block, ones_at(same_parity & (q == px + (TS * j - ix))))


def spectral_blocks(width):
    k = np.arange(width)
    fwd = np.exp(-2j * np.pi * (np.outer(k, k) % width) / width) / np.sqrt(width)
    centred = (k + width // 2) % width - width // 2
    phase = np.exp(-0.2j * centred * centred / width)
    ahead = np.conj(fwd) @ (phase[:, None] * fwd)
    found = []
    for m in (fwd, np.conj(fwd), ahead, np.conj(ahead)):
        full = np.block([[m.real, m.imag], [-m.imag, m.real]]).astype(np.float32)
        high = full.astype(jnp.bfloat16)
        found += [high, (full - high.astype(np.float32)).astype(jnp.bfloat16)]
    return np.stack(found)


def params(**kw):
    return pltpu.CompilerParams(vmem_limit_bytes=32 * 1024 * 1024, **kw)


def row_plan(obj_tiles, tile_map, offsets, probe, intens):
    owners = lax.axis_size("pos")
    layers = lax.axis_size("tile")
    per = obj_tiles.shape[0]
    w = probe.shape[-1]
    bf, f32 = jnp.bfloat16, jnp.float32
    vm = pl.BlockSpec(memory_space=VM)
    sm = pl.BlockSpec(memory_space=SM)
    dma = pltpu.SemaphoreType.DMA
    scalars = (offsets.T, tile_map.T)
    tiles = obj_tiles.reshape(per, 4 * HALF, 2 * TS)
    tables = jnp.asarray(spectral_blocks(w))
    chunk = 2 * w // owners
    gathered, ptotal = pl.pallas_call(
        functools.partial(main_kernel, owners, layers, per, tile_map.shape[0]),
        out_shape=[
            jax.ShapeDtypeStruct((2, layers, owners, 2 * w, w), bf),
            jax.ShapeDtypeStruct((owners, chunk, w), f32),
        ],
        in_specs=[sm, sm, vm, vm, vm, vm],
        out_specs=[vm, vm],
        scratch_shapes=[
            VM((owners, 2 * TS, 2 * w), bf), VM((owners, 2 * TS, 2 * w), bf), VM((2 * w, w), f32),
            VM((owners, chunk, w), f32), VM((chunk, w), f32), VM((layers, chunk, w), f32),
            dma((owners,)), dma((owners,)),
            dma((2, layers, 4)), dma((2, layers, 4)),
            dma((2, 2, layers, 4)), dma((2, 2, layers, 4)),
            dma((2, layers, 4)), dma((2, layers, 4)),
            dma((owners,)), dma((owners,)), dma((layers,)), dma((layers,)), dma((owners,)), dma((owners,)),
        ],
        compiler_params=params(collective_id=0, has_side_effects=True),
    )(*scalars, tiles, probe, intens, tables)
    total = pl.pallas_call(
        functools.partial(add_kernel, owners, layers, per),
        out_shape=jax.ShapeDtypeStruct((per, 4 * HALF, 2 * TS), f32),
        in_specs=[sm, sm, vm],
        out_specs=vm,
        compiler_params=params(),
    )(*scalars, gathered)
    return (total.reshape(per, 4, TS * TS), ptotal.reshape(2, w, w))


def solution(mesh):
    in_specs = (P("pos", None, None), P(), P(), P(), P(("pos", "tile"), None, None))
    out_specs = (P("pos", None, None), P())
    plan = row_plan if mesh.shape["pos"] == OWN_R else general_plan
    return jax.shard_map(plan, mesh=mesh, in_specs=in_specs, out_specs=out_specs, check_vma=False)
```
